512 devices in a mesh: dp: 32 (over x, y), list: 16 (over z, core).
Axes of the slice: x: 4, y: 8, z: 8, core: 2. Of those that a mesh axis runs over, the one named last changes fastest.
Arguments:
- points: bfloat16 [1048576, 1024], P(('dp', 'list')), may hold values from -16 to 16
- block_cluster: int32 [4096], P(('dp', 'list')), may hold values from 0 to 15, as said below
- block_rows: int32 [4096], P(('dp', 'list')), may hold values from 1 to 256, as said below
- coarse: bfloat16 [16, 1024], replicated, may hold values from -16 to 16
- fine: bfloat16 [16, 256, 1024], P('list'), may hold values from -16 to 16
Outputs:
- new_fine: float32 [16, 256, 1024], P('list', 'dp')
- coarse_shift: float32 [16, 1024], P('list')
The draws below stay inside these ranges and needn't reach their ends.
Inputs may be any that keep to these rules, and one draw needn't show every extreme that they name: Within each device's 8 blocks the clusters rise, and no two of them have the same owner block_cluster. `block_rows`: the valid rows of a block come first.
All inputs are finite; a program needn't handle non-finite values.
Results may differ from the reference program's by a relative error of at most 0.006.
Values may be sent and summed in bfloat16 or wider, within the bound.
A program may use at most 128 MiB of HBM per device.

```python
import jax
import jax.numpy as jnp
from jax import lax

VECTOR_DIMENSION = 1024
FINE = 256
BLOCK = 256
BLK_DEV = 8
KC_DEV = 1
KC = 16
NBLK = 4096
ROWS = 1048576


def cluster_ids(base_key):
    seed_all = jax.random.fold_in(base_key, 101)
    seed_pop, seed_score, seed_local = jax.random.split(seed_all, 3)
    owner_count = KC // KC_DEV
    device_count = NBLK // BLK_DEV
    weight = jnp.left_shift(jnp.int32(1), jax.random.randint(seed_pop, (owner_count,), 0, 4))
    membership_logits = jax.random.randint(seed_score, (device_count, owner_count), 0, 1024) * weight[None, :] * owner_count
    membership_logits = membership_logits + jnp.arange(owner_count, dtype=jnp.int32)[None, :]
    _, chosen = lax.top_k(membership_logits, BLK_DEV)
    local_pick = jax.random.randint(seed_local, (device_count, BLK_DEV), 0, KC_DEV)
    labels = jnp.sort(chosen.astype(jnp.int32) * KC_DEV + local_pick, axis=1)
    return labels.reshape(NBLK).astype(jnp.int32)


def coarse_table(base_key):
    seed_one = jax.random.fold_in(base_key, 102)
    return jnp.clip(jax.random.normal(seed_one, (KC, VECTOR_DIMENSION), jnp.float32), -16.0, 16.0)


def drift_table(base_key):
    seed_one = jax.random.fold_in(base_key, 103)
    return 0.5 * jax.random.normal(seed_one, (KC, VECTOR_DIMENSION), jnp.float32)


def fine_table(base_key, spread):
    seed_all = jax.random.fold_in(base_key, 104)
    seed_base, seed_level = jax.random.split(seed_all, 2)
    level = 1.0 + 0.2 * jax.random.randint(seed_level, (KC, 1, 1), 0, 3).astype(jnp.float32)
    values = jax.random.normal(seed_base, (KC, FINE // 2, 2, VECTOR_DIMENSION), jnp.float32)
    even_rows = values[:, :, 0, :]
    odd_rows = values[:, :, 1, :]
    table_all = jnp.stack([even_rows, odd_rows], axis=2).reshape(KC, FINE, VECTOR_DIMENSION)
    return jnp.clip(spread * level * table_all, -16.0, 16.0)


def draw_block_cluster(key, part):
    return cluster_ids(key)


def draw_block_rows(key, part):
    key = jax.random.fold_in(key, 7)
    device_count = NBLK // BLK_DEV
    owner_dev = jnp.arange(NBLK, dtype=jnp.int32) // BLK_DEV
    ceiling = BLOCK - 2 * BLOCK // 3 * (device_count - 1 - owner_dev) // max(device_count - 1, 1)
    drawn = jax.random.randint(key, (NBLK,), 1, ceiling + 1)
    leading = jnp.arange(NBLK, dtype=jnp.int32) % BLK_DEV == 0
    return jnp.where(leading, ceiling, drawn).astype(jnp.int32)


def draw_coarse(key, part):
    return coarse_table(key).astype(jnp.bfloat16)


def draw_fine(key, part):
    return fine_table(key, 0.3).astype(jnp.bfloat16)


def draw_points(key, part):
    labels = cluster_ids(key)
    centres = coarse_table(key)
    drifts = drift_table(key)
    tables = fine_table(key, 0.3)
    seed_all = jax.random.fold_in(key, 9)
    seed_pick, seed_noise = jax.random.split(seed_all, 2)
    picked = jax.random.randint(seed_pick, (NBLK, BLOCK), 0, FINE)

    def one_block(block_index):
        cluster = labels[block_index]
        group_centroid_matrix = lax.dynamic_index_in_dim(tables, cluster, 0, keepdims=False)
        centre = lax.dynamic_index_in_dim(centres, cluster, 0, keepdims=False)
        drift_row = lax.dynamic_index_in_dim(drifts, cluster, 0, keepdims=False)
        choose = picked[block_index]
        seed_here = jax.random.fold_in(seed_noise, block_index)
        noise = 0.5 * jax.random.normal(seed_here, (BLOCK, VECTOR_DIMENSION), jnp.float32)
        values = centre[None, :] + drift_row[None, :] + group_centroid_matrix[choose] + noise
        return jnp.clip(values, -16.0, 16.0)
    every = lax.map(one_block, jnp.arange(NBLK, dtype=jnp.int32))
    return every.reshape(ROWS, VECTOR_DIMENSION).astype(jnp.bfloat16)


def setup_inputs(seed: int = 0) -> dict:
    arg_keys = jax.random.split(jax.random.key(seed), 6)
    points = draw_points(jax.random.fold_in(arg_keys[5], 71), 0)
    block_cluster = draw_block_cluster(jax.random.fold_in(arg_keys[5], 71), 0)
    block_rows = draw_block_rows(jax.random.fold_in(arg_keys[5], 71), 0)
    coarse = draw_coarse(jax.random.fold_in(arg_keys[5], 71), 0)
    fine = draw_fine(jax.random.fold_in(arg_keys[5], 71), 0)
    return dict(points=points, block_cluster=block_cluster, block_rows=block_rows, coarse=coarse, fine=fine)


def reference(points, block_cluster, block_rows, coarse, fine):
    block_count = block_cluster.shape[0]
    smoothing_divisor = VECTOR_DIMENSION / 32.0
    point_rows = points.reshape(block_count, BLOCK, VECTOR_DIMENSION)
    fine_norm = jnp.sum(jnp.square(fine.astype(jnp.float32)), axis=2)
    row_index = jnp.arange(BLOCK, dtype=jnp.int32)

    def absorb(carry, item):
        fine_sums, counts, drift_sum, seen_rows = carry
        block_pts, cluster, valid_rows = item
        centre = lax.dynamic_index_in_dim(coarse, cluster, 0, keepdims=False)
        leftover_offsets = (block_pts.astype(jnp.float32) - centre.astype(jnp.float32)).astype(jnp.bfloat16)
        group_centroid_matrix = lax.dynamic_index_in_dim(fine, cluster, 0, keepdims=False)
        point_magnitudes = lax.dynamic_index_in_dim(fine_norm, cluster, 0, keepdims=False)
        membership_logits = (2.0 * jnp.dot(leftover_offsets, group_centroid_matrix.T, preferred_element_type=jnp.float32) - point_magnitudes[None, :]) / smoothing_divisor
        live_mask = row_index < valid_rows
        highest = jnp.max(membership_logits, axis=1, keepdims=True)
        expo = jnp.exp(membership_logits - highest)
        weights = expo / jnp.sum(expo, axis=1, keepdims=True)
        weights = jnp.where(live_mask[:, None], weights, jnp.float32(0.0))
        weight_half = weights.astype(jnp.bfloat16)
        partial_value = jnp.dot(weight_half.T, leftover_offsets, preferred_element_type=jnp.float32)
        fine_sums = fine_sums.at[cluster].add(partial_value)
        counts = counts.at[cluster].add(jnp.sum(weights, axis=0))
        kept_sum = jnp.sum(jnp.where(live_mask[:, None], leftover_offsets.astype(jnp.float32), jnp.float32(0.0)), axis=0)
        drift_sum = drift_sum.at[cluster].add(kept_sum)
        seen_rows = seen_rows.at[cluster].add(valid_rows.astype(jnp.float32))
        return (fine_sums, counts, drift_sum, seen_rows), None

    start = (jnp.zeros((KC, FINE, VECTOR_DIMENSION), jnp.float32), jnp.zeros((KC, FINE), jnp.float32),
             jnp.zeros((KC, VECTOR_DIMENSION), jnp.float32), jnp.zeros((KC,), jnp.float32))
    carry, _ = lax.scan(absorb, start, (point_rows, block_cluster.astype(jnp.int32), block_rows.astype(jnp.int32)))
    fine_sums, counts, drift_sum, seen_rows = carry
    new_fine = (fine_sums + fine.astype(jnp.float32)) / (counts[:, :, None] + 1.0)
    coarse_shift = drift_sum / (seen_rows[:, None] + 1.0)
    return new_fine, coarse_shift
```

```python
import functools

import jax
import jax.numpy as jnp
from jax import lax
from jax.experimental import pallas as pl
from jax.experimental.pallas import tpu as pltpu
from jax.sharding import PartitionSpec as P

NX, NY, NZ = 4, 8, 8
D, K, B = 1024, 256, 256
SLOTS = 8
OFF = (0, 1, -1, 2, -2, 3, -3, 4)
GROUPS = ((0,), (1, 2), (3, 4), (5, 6), (7,))
AZ0, AZN = 0, 384
AY0, AYN = 384, 256
AX0, AXN = 640, 384
YC, XC = 640, 384
NSEM = 400
RING_AG = (1, 2, 3)
RING_RS = (0, 1, 2, 3)
MESH = pl.DeviceIdType.MESH
BF, F32 = jnp.bfloat16, jnp.float32


def kernel(clus, rows, points, coarse, fine, out, shift,
           pts, res, stage, tab, py, px, ry, rx, szy, szx, rzy, rzx, accy, accx, rfy, rfx,
           rowmsg, rowin, aux, raz, ray, rax, ssem, rsem, lsem):
    dp, li = lax.axis_index("dp"), lax.axis_index("list")
    x, y, z, core = dp // NY, dp % NY, li // 2, li % 2

    def at(dx=0, dy=0, dz=0, dc=0):
        xx = lax.rem(x + dx + NX, NX)
        yy = lax.rem(y + dy + NY, NY)
        zz = lax.rem(z + dz + NZ, NZ)
        return (xx * NY + yy, zz * 2 + lax.rem(core + dc, 2))

    load_pts = pltpu.make_async_copy(points, pts, lsem.at[0])
    load_pts.start()
    load_fine = pltpu.make_async_copy(fine.at[0], tab.at[0], lsem.at[1])
    load_fine.start()

    partners = [dict(dc=1)]
    partners += [dict(dz=d) for d in range(1, NZ)]
    partners += [dict(dy=d) for d in range(1, NY)]
    partners += [dict(dx=d) for d in range(1, NX)]
    barrier = pltpu.get_barrier_semaphore()
    for p in partners:
        pl.semaphore_signal(barrier, inc=1, device_id=at(**p), device_id_type=MESH)

    started = []
    made = {}

    def send(key, src, dst, **to):
        i = len(made)
        c = pltpu.make_async_remote_copy(
            src_ref=src, dst_ref=dst, send_sem=ssem.at[i], recv_sem=rsem.at[i],
            device_id=at(**to), device_id_type=MESH)
        assert key not in made
        made[key] = c
        c.start()
        started.append(c)

    def got(key):
        made[key].wait_recv()

    def got_all(keys):
        for k in keys:
            got(k)

    events = []

    def ev(t, fn, *a):
        events.append((t, len(events), fn, a))

    cents = coarse[...].astype(F32)
    crow = lax.broadcasted_iota(jnp.int32, (16, 1), 0)

    def find(s, parity):
        c = 2 * lax.rem(z + OFF[s] + NZ, NZ) + parity
        b, n = jnp.int32(0), jnp.int32(0)
        for j in range(8):
            hit = clus[j] == c
            b = jnp.where(hit, j, b)
            n = jnp.where(hit, rows[j], n)
        centre = jnp.sum(jnp.where(crow == c, cents, 0.0), axis=0, keepdims=True)
        return b, n, centre

    def residual(s, parity, put):
        b, n, centre = find(s, parity)

        @pl.loop(0, B, step=32)
        def _(r):
            r = pl.multiple_of(r, 32)
            v = pts[b, pl.ds(r, 32), :].astype(F32) - centre
            put[pl.ds(r, 32), :] = v.astype(BF)

        return n

    own_rows = {}

    def send_rows():
        sub = lax.broadcasted_iota(jnp.int32, (8, 128), 0)
        m = jnp.zeros((8, 128), jnp.int32)
        for s in range(SLOTS):
            m = jnp.where(sub == s, find(s, 1 - core)[1], m)
        rowmsg[...] = m
        send("rows", rowmsg, rowin, dc=1)

    def stage_slot(s):
        residual(s, 1 - core, stage.at[s])
        send(("res", s), stage.at[s], res.at[s, pl.ds(B, B)], dc=1)

    def keep_slot(s):
        own_rows[s] = residual(s, core, res.at[s, pl.ds(0, B)])

    def zpieces(s, part):
        h = 2 if part is not None else 1
        q = part or 0
        return (
            ("x", pl.multiple_of(64 * x + q * 32, 32), 64 // h, AX0, AXN),
            ("y", pl.multiple_of(32 * y + q * 16, 16), 32 // h, AY0, AYN),
            ("z", q * 128, 256 // h, AZ0, AZN),
        )

    def zsend(d, way, names):
        s = 0 if d == 1 else OFF.index(way * (d - 1))
        t = 7 if d == 4 else OFF.index(way * d)
        part = None if d < 4 else (0 if way > 0 else 1)
        for name, r0, nr, c0, nc in zpieces(s, part):
            if name in names:
                send(("az", d, way, name), tab.at[s, pl.ds(r0, nr), pl.ds(c0, nc)],
                     tab.at[t, pl.ds(r0, nr), pl.ds(c0, nc)], dz=-way)

    def zhop(d, names):
        for way in (1, -1):
            got_all([("az", d, way, n) for n in names])
            if d < 4:
                zsend(d + 1, way, names)

    def xpiece(s):
        p = tab.at[s, pl.ds(pl.multiple_of(64 * x, 64), 64), pl.ds(AX0, AXN)]
        for j in (2, 1, 3):
            send(("ax", s, j), p, p, dx=j)

    def ydirect(s):
        p = tab.at[s, pl.ds(pl.multiple_of(32 * y, 32), 32), pl.ds(AY0, AYN)]
        for j in (4, 3, 5, 2, 6, 1, 7):
            send(("ayd", s, j), p, p, dy=j)

    def yring(g, h):
        for way in (1, -1):
            sl = GROUPS[g]
            if h == 4:
                sl = sl[:1] if way > 0 else sl[1:]
            if not sl:
                continue
            r0 = pl.multiple_of(32 * lax.rem(y - way * (h - 1) + NY, NY), 32)
            p = tab.at[pl.ds(sl[0], len(sl)), pl.ds(r0, 32), pl.ds(AY0, AYN)]
            send(("ay", g, h, way), p, p, dy=way)

    def yhop(g, h):
        got_all([k for k in (("ay", g, h, 1), ("ay", g, h, -1)) if k in made])
        if h < 4:
            yring(g, h + 1)

    lane = lax.broadcasted_iota(jnp.int32, (1, 128), 1)

    def compute(s):
        r = res.at[s]
        f = tab[s]
        st = lax.dot_general(f, r[...], (((1,), (1,)), ((), ())), preferred_element_type=F32)
        ff = f.astype(F32)
        norm = jnp.sum(ff * ff, axis=1, keepdims=True)
        logits = st * (2.0 / 32.0) - norm * (1.0 / 32.0)
        e = jnp.exp(logits - jnp.max(logits, axis=0, keepdims=True))
        n = own_rows[s]
        n2 = rowin[pl.ds(s, 1), :]
        live = jnp.concatenate([lane < n, lane + 128 < n, lane < n2, lane + 128 < n2], axis=1)
        live = jnp.where(live, 1.0, 0.0)
        w = e * (live / jnp.sum(e, axis=0, keepdims=True))
        wh = w.astype(BF)
        ones = jnp.ones((16, 2 * B), BF)
        cnt = lax.dot_general(ones, wh, (((1,), (1,)), ((), ())), preferred_element_type=F32)
        lhs = jnp.concatenate([wh, jnp.broadcast_to(live, (16, 2 * B)).astype(BF)], axis=0)
        sub = lax.broadcasted_iota(jnp.int32, (8, 128), 0)
        drift = jnp.zeros((8, 128), F32)
        for c0 in range(0, D, 128):
            p = jnp.dot(lhs, r[:, c0:c0 + 128], preferred_element_type=F32)
            drift = jnp.where(sub == c0 // 128, p[K:K + 8], drift)
            if c0 < YC:
                for yy in range(NY):
                    q = jnp.concatenate([p[64 * k + 8 * yy:64 * k + 8 * yy + 8] for k in range(NX)], axis=0)
                    py[s, yy, :, c0:c0 + 128] = q.astype(BF)
            else:
                for xx in range(NX):
                    px[s, xx, :, c0 - YC:c0 - YC + 128] = p[64 * xx:64 * xx + 64].astype(BF)
        seen = jnp.broadcast_to((n + n2).astype(F32), (8, 128))
        more = jnp.where(sub == 0, cnt[:8, :128], jnp.where(sub == 1, cnt[:8, 128:], seen))
        aux[s, 0:8, :] = drift
        aux[s, 8:16, :] = more
        if s:
            send(("auxz", s), aux.at[s], raz.at[s], dz=OFF[s])

    def rs_x(s):
        for j in (2, 1, 3):
            send(("rx", s, j), px.at[s, lax.rem(x + j, NX)], rx.at[s, j - 1], dx=j)

    def rs_x_done(s):
        got_all([("rx", s, j) for j in (1, 2, 3)])
        v = px[s, x].astype(F32)
        for j in range(3):
            v = v + rx[s, j].astype(F32)
        if s == 0:
            accx[...] = v.reshape(NY, 8, XC)
        else:
            szx[s] = v.astype(BF)
            send(("zx", s), szx.at[s], rzx.at[s], dz=OFF[s])

    def rs_y_send(g, dist):
        for way in (1, -1):
            sl = GROUPS[g]
            if dist == 4:
                sl = sl[:1] if way > 0 else sl[1:]
            if not sl:
                continue
            to = lax.rem(y + way * dist + NY, NY)
            send(("ry", g, dist, way), py.at[pl.ds(sl[0], len(sl)), to],
                 ry.at[(way < 0) * 4 + dist - 1, pl.ds(sl[0], len(sl))], dy=way)

    def rs_y_hop(g, dist):
        for way in (1, -1):
            if ("ry", g, dist, way) not in made:
                continue
            sl = GROUPS[g]
            if dist == 4:
                sl = sl[:1] if way > 0 else sl[1:]
            got(("ry", g, dist, way))
            to = lax.rem(y + way * (dist - 1) + NY, NY)
            for s in sl:
                v = py[s, to].astype(F32) + ry[(way < 0) * 4 + dist - 1, s].astype(F32)
                py[s, to] = v.astype(BF)
        rs_y_send(g, dist - 1)

    def rs_y_out(s, v):
        if s == 0:
            accy[...] = v.reshape(NX, 8, YC)
        else:
            szy[s] = v.astype(BF)
            send(("zy", s), szy.at[s], rzy.at[s], dz=OFF[s])

    def rs_y_done(g):
        got_all([("ry", g, 1, 1), ("ry", g, 1, -1)])
        for s in GROUPS[g]:
            rs_y_out(s, py[s, y].astype(F32) + ry[0, s].astype(F32) + ry[4, s].astype(F32))

    def rs_y_direct(s):
        for j in (4, 3, 5, 2, 6, 1, 7):
            send(("ryd", s, j), py.at[s, lax.rem(y + j, NY)], ry.at[j - 1, s], dy=j)

    def rs_y_direct_done(s):
        v = py[s, y].astype(F32)
        for j in range(1, 8):
            got(("ryd", s, j))
            v = v + ry[j - 1, s].astype(F32)
        rs_y_out(s, v)

    def add_z(s):
        got(("zy", s))
        accy[...] += rzy[s].astype(F32).reshape(NX, 8, YC)
        got(("zx", s))
        accx[...] += rzx[s].astype(F32).reshape(NY, 8, XC)

    def last_send():
        for j in (2, 1, 3):
            send(("fy", j), accy.at[lax.rem(x + j, NX)], rfy.at[j - 1], dx=j)
        for j in (4, 3, 5, 2, 6, 1, 7):
            send(("fx", j), accx.at[lax.rem(y + j, NY)], rfx.at[j - 1], dy=j)

    def aux_z():
        v = aux[0]
        for s in range(1, SLOTS):
            got(("auxz", s))
            v = v + raz[s]
        raz[0] = v
        ray[y] = v
        for j in (4, 3, 5, 2, 6, 1, 7):
            send(("auxy", j), raz.at[0], ray.at[y], dy=j)

    def aux_y():
        got_all([("auxy", j) for j in range(1, NY)])
        v = ray[0]
        for j in range(1, NY):
            v = v + ray[j]
        aux[0] = v
        rax[x] = v
        for j in (2, 1, 3):
            send(("auxx", j), aux.at[0], rax.at[x], dx=j)

    def aux_x():
        got_all([("auxx", j) for j in range(1, NX)])
        v = rax[0]
        for j in range(1, NX):
            v = v + rax[j]
        seen = v[10:11, :]
        d = v[0:8] / (seen + 1.0)
        for i in range(8):
            shift[:, 128 * i:128 * i + 128] = d[i:i + 1]
        k0 = lax.rem(dp, 16) * 8
        line = jnp.where(dp < 16, v[8:9], v[9:10])
        pick = lax.broadcasted_iota(jnp.int32, (8, 128), 1) == k0 + lax.broadcasted_iota(jnp.int32, (8, 128), 0)
        made["cnt"] = jnp.sum(jnp.where(pick, jnp.broadcast_to(line, (8, 128)), 0.0), axis=1, keepdims=True)

    def finish():
        old = tab[0, pl.ds(pl.multiple_of((dp // 2) * 16, 16), 16), :].astype(F32)
        old = jnp.where(lax.rem(dp, 2) == 0, old[:8], old[8:])
        vy = accy[x]
        for j in (1, 2, 3):
            got(("fy", j))
            vy = vy + rfy[j - 1]
        div = made["cnt"] + 1.0
        out[0, :, :YC] = (vy + old[:, :YC]) / div
        vx = accx[y]
        for j in range(1, NY):
            got(("fx", j))
            vx = vx + rfx[j - 1]
        out[0, :, YC:] = (vx + old[:, YC:]) / div

    hz, hzz, hx, hy, hr = 3.2, 4.2, 4.0, 2.3, 2.7
    for way in (1, -1):
        ev(0.0, zsend, 1, way, "xy")
    for way in (1, -1):
        ev(0.01, zsend, 1, way, "z")
    ev(0.05, load_pts.wait)
    ev(0.1, send_rows)
    for s in range(SLOTS):
        ev(0.2 + 0.7 * s, stage_slot, s)
        ev(0.5 + 0.7 * s, keep_slot, s)
    ready = {0: 2.6}
    for d in range(1, 5):
        g = d
        ev(hz * d, zhop, d, "xy")
        ev(max(hzz * d, hz * d + 0.1), zhop, d, "z")
        for s in GROUPS[g]:
            ev(hz * d + 0.01, xpiece, s)
            ev(hz * d + hx, got_all, [("ax", s, j) for j in (1, 2, 3)])
        if g in RING_AG:
            ev(hz * d + 0.02, yring, g, 1)
            for h in range(1, 5):
                ev(hz * d + hy * h, yhop, g, h)
            ready[g] = max(hz * d + hy * 4, hzz * d, hz * d + hx) + 0.02
        else:
            for s in GROUPS[g]:
                ev(hz * d + 0.02, ydirect, s)
                ev(hz * d + 5.0, got_all, [("ayd", s, j) for j in range(1, 8)])
            ready[g] = max(hz * d + 5.0, hzz * d, hz * d + hx) + 0.02
    busy = 0.0
    last = 0.0
    for g in range(5):
        t = max(ready[g], busy)
        for s in GROUPS[g]:
            if s == 0:
                ev(t - 0.01, got, "rows")
            ev(t, got, ("res", s))
            ev(t, compute, s)
            t += 1.0
            ev(t, rs_x, s)
        busy = t
        if g in RING_RS:
            ev(t, rs_y_send, g, 4)
            for dist in range(4, 1, -1):
                if dist == 4:
                    ev(t + hr, rs_y_hop, g, 4)
                else:
                    ev(t + hr * (5 - dist), rs_y_hop, g, dist)
            ev(t + hr * 4, rs_y_done, g)
            tz = t + hr * 4
        else:
            for s in GROUPS[g]:
                ev(t + 0.01, rs_y_direct, s)
                ev(t + 6.0, rs_y_direct_done, s)
            tz = t + 6.0
        for s in GROUPS[g]:
            ev(t + 4.0, rs_x_done, s)
            if s:
                ev(max(tz, last) + 4.2, add_z, s)
        last = max(last, tz)
    ev(busy + 4.0, aux_z)
    ev(busy + 8.0, aux_y)
    ev(busy + 11.0, aux_x)
    ev(last + 4.6, last_send)
    ev(last + 8.0, finish)

    load_fine.wait()
    pl.semaphore_wait(barrier, len(partners))
    for _, _, fn, a in sorted(events, key=lambda e: e[:2]):
        fn(*a)
    for c in started:
        c.wait_send()


def per_device(points, block_cluster, block_rows, coarse, fine):
    vmem = pl.BlockSpec(memory_space=pltpu.VMEM)
    smem = pl.BlockSpec(memory_space=pltpu.SMEM)
    hbm = pl.BlockSpec(memory_space=pl.ANY)
    return pl.pallas_call(
        kernel,
        out_shape=(jax.ShapeDtypeStruct((1, 8, D), F32), jax.ShapeDtypeStruct((1, D), F32)),
        in_specs=[smem, smem, hbm, vmem, hbm],
        out_specs=(vmem, vmem),
        scratch_shapes=[
            pltpu.VMEM((8, B, D), BF),
            pltpu.VMEM((SLOTS, 2 * B, D), BF),
            pltpu.VMEM((SLOTS, B, D), BF),
            pltpu.VMEM((SLOTS, K, D), BF),
            pltpu.VMEM((SLOTS, NY, 32, YC), BF),
            pltpu.VMEM((SLOTS, NX, 64, XC), BF),
            pltpu.VMEM((8, SLOTS, 32, YC), BF),
            pltpu.VMEM((SLOTS, 3, 64, XC), BF),
            pltpu.VMEM((SLOTS, 32, YC), BF),
            pltpu.VMEM((SLOTS, 64, XC), BF),
            pltpu.VMEM((SLOTS, 32, YC), BF),
            pltpu.VMEM((SLOTS, 64, XC), BF),
            pltpu.VMEM((NX, 8, YC), F32),
            pltpu.VMEM((NY, 8, XC), F32),
            pltpu.VMEM((NX - 1, 8, YC), F32),
            pltpu.VMEM((NY - 1, 8, XC), F32),
            pltpu.VMEM((8, 128), jnp.int32),
            pltpu.VMEM((8, 128), jnp.int32),
            pltpu.VMEM((SLOTS, 16, 128), F32),
            pltpu.VMEM((SLOTS, 16, 128), F32),
            pltpu.VMEM((NY, 16, 128), F32),
            pltpu.VMEM((NX, 16, 128), F32),
            pltpu.SemaphoreType.DMA((NSEM,)),
            pltpu.SemaphoreType.DMA((NSEM,)),
            pltpu.SemaphoreType.DMA((2,)),
        ],
        compiler_params=pltpu.CompilerParams(
            collective_id=0, has_side_effects=True, vmem_limit_bytes=56 * 1024 * 1024),
        cost_estimate=pl.CostEstimate(flops=8 * 10**9, bytes_accessed=5 * 10**6, transcendentals=10**6),
        name="lloyd",
    )(block_cluster, block_rows, points.reshape(8, B, D), coarse, fine)


def solution(mesh):
    placed = (
        P(("dp", "list"), None),
        P(("dp", "list")),
        P(("dp", "list")),
        P(),
        P("list", None, None),
    )
    return jax.shard_map(
        per_device,
        mesh=mesh,
        in_specs=placed,
        out_specs=(P("list", "dp", None), P("list", None)),
        check_vma=False,
    )
```

```python
import functools

import jax
import jax.numpy as jnp
from jax import lax
from jax.experimental import pallas as pl
from jax.experimental.pallas import tpu as pltpu
from jax.sharding import PartitionSpec as P

NX, NY, NZ = 4, 8, 8
D, K, B = 1024, 256, 256
SLOTS = 8
OFF = (0, 1, -1, 2, -2, 3, -3, 4)
GROUPS = ((0,), (1, 2), (3, 4), (5, 6), (7,))
AZ0, AZN = 0, 512
AX0, AXN = 512, 512
FAR = (5, 6, 7)
H = D // 2
NSEM = 400
MESH = pl.DeviceIdType.MESH
BF, F32 = jnp.bfloat16, jnp.float32
ORDER = (
    ("zs", 1, -1, "x"), ("zs", 1, 1, "x"), ("zs", 1, -1, 0), ("zs", 1, 1, 0), ("zs", 1, 1, 1), ("zs", 1, -1, 1),
    ("pts",), ("stage", 0), ("stage", 1), ("keep", 0), ("keep", 1), ("stage", 2), ("stage", 3), ("keep", 2),
    ("keep", 3), ("stage", 4), ("stage", 5), ("xp", 1), ("zf", 1, -1, "x"), ("zf", 1, 1, "x"), ("keep", 4),
    ("keep", 5), ("stage", 6), ("stage", 7), ("keep", 6), ("keep", 7), ("zf", 1, -1, 0), ("zf", 1, 1, 0), ("comp", 0),
    ("ry", 0, 4), ("xp", 2), ("zf", 1, -1, 1), ("zf", 1, 1, 1), ("comp", 1), ("xp", 3), ("xp", 4), ("zf", 2, -1, "x"),
    ("zf", 2, 1, "x"), ("ry", 0, 3), ("zf", 2, -1, 0), ("zf", 2, 1, 0), ("comp", 2), ("ry", 1, 4), ("zf", 2, 1, 1),
    ("zf", 2, -1, 1), ("ry", 0, 2), ("zf", 3, 1, "x"), ("xp", 5), ("zf", 3, -1, "x"), ("xp", 6), ("comp", 3),
    ("ry", 1, 3), ("zf", 3, -1, 0), ("zf", 3, 1, 0), ("comp", 4), ("ry", 0, 1), ("ry", 2, 4), ("zf", 3, -1, 1),
    ("zf", 3, 1, 1), ("xp", 7), ("comp", 5), ("ry", 1, 2), ("comp", 6), ("ryd", 0), ("ry", 2, 3), ("comp", 7),
    ("ry", 1, 1), ("ry", 2, 2), ("rxd", 5), ("auxz",), ("ryd", 1), ("ry", 2, 1), ("rxd", 6), ("addz", 2), ("addz", 1),
    ("bdone", 5), ("auxy",), ("rxd", 7), ("ryd", 2), ("auxx",), ("bdone", 6), ("addz", 4), ("addz", 3), ("last",),
    ("bdone", 7), ("finish",),
)

def kernel(clus, rows, points, coarse, fine, out,
           pts, res, stage, tab, py, px, ry, rx, szy, rzy, sbx, rbx, szc, rzc, accy, rfy,
           rowmsg, rowin, aux, raz, ray, rax, ssem, rsem, lsem):
    dp, li = lax.axis_index("dp"), lax.axis_index("list")
    x, y, z, core = dp // NY, dp % NY, li // 2, li % 2

    def at(dx=0, dy=0, dz=0, dc=0):
        xx = lax.rem(x + dx + NX, NX)
        yy = lax.rem(y + dy + NY, NY)
        zz = lax.rem(z + dz + NZ, NZ)
        return (xx * NY + yy, zz * 2 + lax.rem(core + dc, 2))

    load_pts = pltpu.make_async_copy(points, pts, lsem.at[0])
    load_pts.start()
    load_fine = pltpu.make_async_copy(fine.at[0], tab.at[0], lsem.at[1])
    load_fine.start()

    partners = [dict(dc=1)]
    partners += [dict(dz=d) for d in range(1, NZ)]
    partners += [dict(dy=d) for d in range(1, NY)]
    partners += [dict(dx=d) for d in range(1, NX)]
    barrier = pltpu.get_barrier_semaphore()
    for p in partners:
        pl.semaphore_signal(barrier, inc=1, device_id=at(**p), device_id_type=MESH)

    started = []
    made = {}
    sent = 0

    def send(key, src, dst, **to):
        i = len(made)
        c = pltpu.make_async_remote_copy(
            src_ref=src, dst_ref=dst, send_sem=ssem.at[i], recv_sem=rsem.at[i],
            device_id=at(**to), device_id_type=MESH)
        assert key not in made
        made[key] = c
        c.start()
        started.append(c)

    waited = set()

    def got(key):
        if key not in waited:
            waited.add(key)
            made[key].wait_recv()

    def got_all(keys):
        for k in keys:
            got(k)

    def group_of(s):
        return [s in g for g in GROUPS].index(True)

    cents = coarse[...].astype(F32)
    crow = lax.broadcasted_iota(jnp.int32, (16, 1), 0)

    def find(s, parity):
        c = 2 * lax.rem(z + OFF[s] + NZ, NZ) + parity
        b, n = jnp.int32(0), jnp.int32(0)
        for j in range(8):
            hit = clus[j] == c
            b = jnp.where(hit, j, b)
            n = jnp.where(hit, rows[j], n)
        centre = jnp.sum(jnp.where(crow == c, cents, 0.0), axis=0, keepdims=True)
        return b, n, centre

    def residual(s, parity, put):
        b, n, centre = find(s, parity)

        @pl.loop(0, B, step=32)
        def _(r):
            r = pl.multiple_of(r, 32)
            v = pts[b, pl.ds(r, 32), :].astype(F32) - centre
            put[pl.ds(r, 32), :] = v.astype(BF)

        return n

    own_rows = {}

    def send_rows():
        sub = lax.broadcasted_iota(jnp.int32, (8, 128), 0)
        m = jnp.zeros((8, 128), jnp.int32)
        for s in range(SLOTS):
            m = jnp.where(sub == s, find(s, 1 - core)[1], m)
        rowmsg[...] = m
        send("rows", rowmsg, rowin, dc=1)

    def stage_slot(s):
        residual(s, 1 - core, stage.at[s])
        send(("res", s), stage.at[s], res.at[s, pl.ds(B, B)], dc=1)

    def keep_slot(s):
        own_rows[s] = residual(s, core, res.at[s, pl.ds(0, B)])

    def zsend(d, way, name):
        s = 0 if d == 1 else OFF.index(way * (d - 1))
        t = 7 if d == 4 else OFF.index(way * d)
        if name == "x":
            half = 32 if d == 4 and way < 0 else 0
            r0, nr, c0, nc = pl.multiple_of(64 * x + half, 32), 32 if d == 4 else 64, AX0, AXN
        else:
            if d == 4 and (name == 0) != (way > 0):
                return
            r0, nr, c0, nc = 128 * name, 128, AZ0, AZN
        send(("az", d, way, name), tab.at[s, pl.ds(r0, nr), pl.ds(c0, nc)],
             tab.at[t, pl.ds(r0, nr), pl.ds(c0, nc)], dz=-way)

    def zhop(d, way, name):
        got(("az", d, way, name))
        zsend(d + 1, way, name)

    def znear(s, name):
        if s == 7:
            got_all([("az", 4, way, name) for way in (1, -1) if ("az", 4, way, name) in made])
        else:
            got(("az", abs(OFF[s]), 1 if OFF[s] > 0 else -1, name))

    def xdirect(s):
        znear(s, "x")
        p = tab.at[s, pl.ds(pl.multiple_of(64 * x, 64), 64), pl.ds(AX0, AXN)]
        for j in (2, 1, 3):
            send(("ax", s, j), p, p, dx=j)

    def table_ready(s):
        if s == 0:
            return
        znear(s, 0)
        znear(s, 1)
        got_all([("ax", s, j) for j in (1, 2, 3)])

    lane = lax.broadcasted_iota(jnp.int32, (1, 128), 1)

    def compute(s):
        table_ready(s)
        if s == 0:
            got("rows")
        got(("res", s))
        r = res.at[s]
        f = tab[s]
        st = lax.dot_general(f, r[...], (((1,), (1,)), ((), ())), preferred_element_type=F32)
        ff = f.astype(F32)
        norm = jnp.sum(ff * ff, axis=1, keepdims=True)
        logits = st * (2.0 / 32.0) - norm * (1.0 / 32.0)
        e = jnp.exp(logits - jnp.max(logits, axis=0, keepdims=True))
        n = own_rows[s]
        n2 = rowin[pl.ds(s, 1), :]
        live = jnp.concatenate([lane < n, lane + 128 < n, lane < n2, lane + 128 < n2], axis=1)
        live = jnp.where(live, 1.0, 0.0)
        w = e * (live / jnp.sum(e, axis=0, keepdims=True))
        wh = w.astype(BF)
        ones = jnp.ones((16, 2 * B), BF)
        cnt = lax.dot_general(ones, wh, (((1,), (1,)), ((), ())), preferred_element_type=F32)
        lhs = jnp.concatenate([wh, jnp.broadcast_to(live, (16, 2 * B)).astype(BF)], axis=0)
        sub = lax.broadcasted_iota(jnp.int32, (8, 128), 0)
        drift = jnp.zeros((8, 128), F32)
        for c0 in range(0, D, 128):
            p = jnp.dot(lhs, r[:, c0:c0 + 128], preferred_element_type=F32)
            drift = jnp.where(sub == c0 // 128, p[K:K + 8], drift)
            if s not in FAR:
                for yy in range(NY):
                    q = jnp.concatenate([p[64 * k + 8 * yy:64 * k + 8 * yy + 8] for k in range(NX)], axis=0)
                    py[s, yy, :, c0:c0 + 128] = q.astype(BF)
            else:
                for xx in range(NX):
                    px[s - FAR[0], xx, :, c0:c0 + 128] = p[64 * xx:64 * xx + 64].astype(BF)
        seen = jnp.broadcast_to((n + n2).astype(F32), (8, 128))
        more = jnp.where(sub == 0, cnt[:8, :128], jnp.where(sub == 1, cnt[:8, 128:], seen))
        aux[s, 0:8, :] = drift
        aux[s, 8:16, :] = more
        if s:
            send(("auxz", s), aux.at[s], raz.at[s], dz=OFF[s])
        if s in FAR:
            rs_x(s - FAR[0])

    def rs_x(f):
        for j in (2, 1, 3):
            send(("rx", f, j), px.at[f, lax.rem(x + j, NX)], rx.at[f, j - 1], dx=j)

    def rs_x_done(f):
        v = px[f, x].astype(F32)
        for j in (1, 3, 2):
            got(("rx", f, j))
            v = v + rx[f, j - 1].astype(F32)
        for yy in range(NY):
            w = v[8 * yy:8 * yy + 8]
            sbx[f, yy] = jnp.concatenate([w[:, :H], w[:, H:]], axis=0).astype(BF)
        for j in (4, 3, 5, 2, 6, 1, 7):
            send(("bx", f, j), sbx.at[f, lax.rem(y + j, NY)], rbx.at[f, j - 1], dy=j)

    def rs_far_done(f):
        v = sbx[f, y].astype(F32)
        for j in range(1, NY):
            got(("bx", f, j))
            v = v + rbx[f, j - 1].astype(F32)
        szc[f] = v
        send(("zc", f), szc.at[f], rzc.at[f], dz=OFF[f + FAR[0]])

    def rs_y_send(g, dist):
        for way in (1, -1):
            sl = GROUPS[g]
            if dist == 4:
                sl = sl[:1] if way > 0 else sl[1:]
            if not sl:
                continue
            to = lax.rem(y + way * dist + NY, NY)
            send(("ry", g, dist, way), py.at[pl.ds(sl[0], len(sl)), to],
                 ry.at[(way < 0) * 4 + dist - 1, pl.ds(sl[0], len(sl))], dy=way)

    def rs_y_hop(g, dist):
        for way in (1, -1):
            if ("ry", g, dist, way) not in made:
                continue
            sl = GROUPS[g]
            if dist == 4:
                sl = sl[:1] if way > 0 else sl[1:]
            got(("ry", g, dist, way))
            to = lax.rem(y + way * (dist - 1) + NY, NY)
            for s in sl:
                v = py[s, to].astype(F32) + ry[(way < 0) * 4 + dist - 1, s].astype(F32)
                py[s, to] = v.astype(BF)
        rs_y_send(g, dist - 1)

    def rs_y_out(s, v):
        if s == 0:
            accy[...] = v.reshape(NX, 8, D)
        else:
            szy[s] = v.astype(BF)
            send(("zy", s), szy.at[s], rzy.at[s], dz=OFF[s])

    def rs_y_done(g):
        got_all([("ry", g, 1, 1), ("ry", g, 1, -1)])
        for s in GROUPS[g]:
            rs_y_out(s, py[s, y].astype(F32) + ry[0, s].astype(F32) + ry[4, s].astype(F32))

    def add_z(s):
        got(("zy", s))
        accy[...] += rzy[s].astype(F32).reshape(NX, 8, D)

    def last_send():
        for j in (2, 1, 3):
            send(("fy", j), accy.at[lax.rem(x + j, NX)], rfy.at[j - 1], dx=j)

    def aux_z():
        v = aux[0]
        for s in range(1, SLOTS):
            got(("auxz", s))
            v = v + raz[s]
        raz[0] = v
        ray[y] = v
        for j in (4, 3, 5, 2, 6, 1, 7):
            send(("auxy", j), raz.at[0], ray.at[y], dy=j)

    def aux_y():
        got_all([("auxy", j) for j in range(1, NY)])
        v = ray[0]
        for j in range(1, NY):
            v = v + ray[j]
        aux[0] = v
        rax[x] = v
        for j in (2, 1, 3):
            send(("auxx", j), aux.at[0], rax.at[x], dx=j)

    def aux_x():
        got_all([("auxx", j) for j in range(1, NX)])
        v = rax[0]
        for j in range(1, NX):
            v = v + rax[j]
        seen = v[10:11, :]
        d = v[0:8] / (seen + 1.0)
        for i in range(8):
            out[8:9, 128 * i:128 * i + 128] = d[i:i + 1]
        k0 = lax.rem(dp, 16) * 8
        line = jnp.where(dp < 16, v[8:9], v[9:10])
        pick = lax.broadcasted_iota(jnp.int32, (8, 128), 1) == k0 + lax.broadcasted_iota(jnp.int32, (8, 128), 0)
        made["cnt"] = jnp.sum(jnp.where(pick, jnp.broadcast_to(line, (8, 128)), 0.0), axis=1, keepdims=True)

    def finish():
        nonlocal sent
        sent = len(started) - 8
        for c in started[:sent]:
            c.wait_send()
        old = tab[0, pl.ds(pl.multiple_of((dp // 2) * 16, 16), 16), :].astype(F32)
        old = jnp.where(lax.rem(dp, 2) == 0, old[:8], old[8:])
        v = old + accy[x]
        for j in (1, 3, 2):
            got(("fy", j))
            v = v + rfy[j - 1]
        got(("zc", 0))
        far = rzc[0]
        for f in range(1, len(FAR)):
            got(("zc", f))
            far = far + rzc[f]
        div = made["cnt"] + 1.0
        out[:8, :H] = (v[:, :H] + far[:8]) / div
        out[:8, H:] = (v[:, H:] + far[8:]) / div

    def run(kind, *a):
        if kind == "pts":
            load_pts.wait()
            send_rows()
        elif kind == "zs":
            zsend(*a)
        elif kind == "zf":
            zhop(*a)
        elif kind == "xp":
            xdirect(*a)
        elif kind == "stage":
            stage_slot(*a)
        elif kind == "keep":
            keep_slot(*a)
        elif kind == "comp":
            compute(*a)
        elif kind == "rxd":
            rs_x_done(a[0] - FAR[0])
        elif kind == "bdone":
            rs_far_done(a[0] - FAR[0])
        elif kind == "ry":
            if a[1] == 4:
                rs_y_send(*a)
            else:
                rs_y_hop(a[0], a[1] + 1)
        elif kind == "ryd":
            rs_y_done(*a)
        elif kind == "addz":
            add_z(*a)
        elif kind == "auxz":
            aux_z()
        elif kind == "auxy":
            aux_y()
        elif kind == "auxx":
            aux_x()
        elif kind == "last":
            last_send()
        elif kind == "finish":
            finish()

    load_fine.wait()
    pl.semaphore_wait(barrier, len(partners))
    for e in ORDER:
        run(*e)
    for c in started[sent:]:
        c.wait_send()


def per_device(points, block_cluster, block_rows, coarse, fine):
    vmem = pl.BlockSpec(memory_space=pltpu.VMEM)
    smem = pl.BlockSpec(memory_space=pltpu.SMEM)
    hbm = pl.BlockSpec(memory_space=pl.ANY)
    far, near = len(FAR), SLOTS - len(FAR)
    both = pl.pallas_call(
        kernel,
        out_shape=jax.ShapeDtypeStruct((16, D), F32),
        in_specs=[smem, smem, hbm, vmem, hbm],
        out_specs=vmem,
        scratch_shapes=[
            pltpu.VMEM((8, B, D), BF),
            pltpu.VMEM((SLOTS, 2 * B, D), BF),
            pltpu.VMEM((SLOTS, B, D), BF),
            pltpu.VMEM((SLOTS, K, D), BF),
            pltpu.VMEM((near, NY, 32, D), BF),
            pltpu.VMEM((far, NX, 64, D), BF),
            pltpu.VMEM((8, near, 32, D), BF),
            pltpu.VMEM((far, NX - 1, 64, D), BF),
            pltpu.VMEM((near, 32, D), BF),
            pltpu.VMEM((near, 32, D), BF),
            pltpu.VMEM((far, NY, 16, H), BF),
            pltpu.VMEM((far, NY - 1, 16, H), BF),
            pltpu.VMEM((far, 16, H), F32),
            pltpu.VMEM((far, 16, H), F32),
            pltpu.VMEM((NX, 8, D), F32),
            pltpu.VMEM((NX - 1, 8, D), F32),
            pltpu.VMEM((8, 128), jnp.int32),
            pltpu.VMEM((8, 128), jnp.int32),
            pltpu.VMEM((SLOTS, 16, 128), F32),
            pltpu.VMEM((SLOTS, 16, 128), F32),
            pltpu.VMEM((NY, 16, 128), F32),
            pltpu.VMEM((NX, 16, 128), F32),
            pltpu.SemaphoreType.DMA((NSEM,)),
            pltpu.SemaphoreType.DMA((NSEM,)),
            pltpu.SemaphoreType.DMA((2,)),
        ],
        compiler_params=pltpu.CompilerParams(
            collective_id=0, has_side_effects=True, vmem_limit_bytes=56 * 1024 * 1024),
        cost_estimate=pl.CostEstimate(flops=8 * 10**9, bytes_accessed=5 * 10**6, transcendentals=10**6),
        name="lloyd",
    )(block_cluster, block_rows, points.reshape(8, B, D), coarse, fine)
    return both[:8].reshape(1, 8, D), both[8:9]


def solution(mesh):
    placed = (
        P(("dp", "list"), None),
        P(("dp", "list")),
        P(("dp", "list")),
        P(),
        P("list", None, None),
    )
    return jax.shard_map(
        per_device,
        mesh=mesh,
        in_specs=placed,
        out_specs=(P("list", "dp", None), P("list", None)),
        check_vma=False,
    )
```

```python
import functools

import jax
import jax.numpy as jnp
from jax import lax
from jax.experimental import pallas as pl
from jax.experimental.pallas import tpu as pltpu
from jax.sharding import PartitionSpec as P

NX, NY, NZ = 4, 8, 8
D, K, B = 1024, 256, 256
SLOTS = 8
OFF = (0, 1, -1, 2, -2, 3, -3, 4)
GROUPS = ((0,), (1, 2), (3, 4), (5, 6), (7,))
AZ0, AZN = 0, 512
AX0, AXN = 512, 512
FAR = (5, 6, 7)
H = D // 2
EARLY = (0, 1, 2)
NSEM = 400
MESH = pl.DeviceIdType.MESH
BF, F32 = jnp.bfloat16, jnp.float32
ORDER = (
    ("zs", 1, -1, "x"), ("zs", 1, 1, "x"), ("zs", 1, -1, 1), ("zs", 1, 1, 1), ("pts",), ("stage", 0), ("stage", 1),
    ("stage", 2), ("keep", 0), ("keep", 1), ("stage", 3), ("keep", 2), ("keep", 3), ("stage", 4), ("stage", 5),
    ("keep", 4), ("keep", 5), ("stage", 6), ("stage", 7), ("keep", 6), ("keep", 7), ("xp", 2), ("zf", 1, 1, "x"),
    ("zf", 1, -1, "x"), ("xp", 1), ("zs", 1, -1, 0), ("comp", 0), ("ry", 0, 4), ("zs", 1, 1, 0), ("zf", 1, -1, 1),
    ("zf", 1, 1, 1), ("xp", 3), ("zf", 2, -1, "x"), ("xp", 4), ("zf", 2, 1, "x"), ("ry", 0, 3), ("zf", 1, -1, 0),
    ("comp", 2), ("zf", 1, 1, 0), ("comp", 1), ("ry", 1, 4), ("zf", 2, 1, 1), ("zf", 2, -1, 1), ("ry", 0, 2),
    ("xp", 6), ("zf", 3, -1, "x"), ("zf", 3, 1, "x"), ("xp", 5), ("zf", 2, -1, 0), ("ry", 1, 3), ("comp", 4),
    ("ry", 0, 1), ("comp", 3), ("ry", 2, 4), ("zf", 3, -1, 1), ("zf", 2, 1, 0), ("xp", 7), ("ry", 1, 2), ("comp", 6),
    ("ryd", 0), ("ry", 2, 3), ("comp", 5), ("zf", 3, 1, 0), ("ry", 1, 1), ("ry", 2, 2), ("comp", 7), ("rxd", 6),
    ("ryd", 1), ("ry", 2, 1), ("auxz",), ("addz", 2), ("rxd", 5), ("addz", 1), ("bdone", 6), ("ryd", 2), ("rxd", 7),
    ("auxy",), ("bdone", 5), ("addz", 3), ("addz", 4), ("last",), ("auxx",), ("bdone", 7), ("finish",),
)

def kernel(clus, rows, points, coarse, fine, out,
           pts, res, stage, tab, py, px, ry, rx, szy, rzy, sbx, rbx, szc, rzc, accy, rfy,
           rowmsg, rowin, aux, raz, ray, rax, ssem, rsem, lsem):
    dp, li = lax.axis_index("dp"), lax.axis_index("list")
    x, y, z, core = dp // NY, dp % NY, li // 2, li % 2

    def at(dx=0, dy=0, dz=0, dc=0):
        xx = lax.rem(x + dx + NX, NX)
        yy = lax.rem(y + dy + NY, NY)
        zz = lax.rem(z + dz + NZ, NZ)
        return (xx * NY + yy, zz * 2 + lax.rem(core + dc, 2))

    load_pts = pltpu.make_async_copy(points, pts, lsem.at[0])
    load_pts.start()
    load_fine = pltpu.make_async_copy(fine.at[0], tab.at[0], lsem.at[1])
    load_fine.start()

    partners = [dict(dc=1)]
    partners += [dict(dz=d) for d in range(1, NZ)]
    partners += [dict(dy=d) for d in range(1, NY)]
    partners += [dict(dx=d) for d in range(1, NX)]
    barrier = pltpu.get_barrier_semaphore()
    for p in partners:
        pl.semaphore_signal(barrier, inc=1, device_id=at(**p), device_id_type=MESH)

    started = []
    made = {}
    sent = 0

    def send(key, src, dst, **to):
        i = len(made)
        c = pltpu.make_async_remote_copy(
            src_ref=src, dst_ref=dst, send_sem=ssem.at[i], recv_sem=rsem.at[i],
            device_id=at(**to), device_id_type=MESH)
        assert key not in made
        made[key] = c
        c.start()
        started.append(c)

    waited = set()

    def got(key):
        if key not in waited:
            waited.add(key)
            made[key].wait_recv()

    def got_all(keys):
        for k in keys:
            got(k)

    def group_of(s):
        return [s in g for g in GROUPS].index(True)

    cents = coarse[...].astype(F32)
    crow = lax.broadcasted_iota(jnp.int32, (16, 1), 0)

    def find(s, parity):
        c = 2 * lax.rem(z + OFF[s] + NZ, NZ) + parity
        b, n = jnp.int32(0), jnp.int32(0)
        for j in range(8):
            hit = clus[j] == c
            b = jnp.where(hit, j, b)
            n = jnp.where(hit, rows[j], n)
        centre = jnp.sum(jnp.where(crow == c, cents, 0.0), axis=0, keepdims=True)
        return b, n, centre

    def residual(s, parity, put):
        b, n, centre = find(s, parity)

        @pl.loop(0, B, step=32)
        def _(r):
            r = pl.multiple_of(r, 32)
            v = pts[b, pl.ds(r, 32), :].astype(F32) - centre
            put[pl.ds(r, 32), :] = v.astype(BF)

        return n

    own_rows = {}

    def fill_rows():
        sub = lax.broadcasted_iota(jnp.int32, (8, 128), 0)
        m = jnp.zeros((8, 128), jnp.int32)
        for s in range(SLOTS):
            m = jnp.where(sub == s, find(s, 1 - core)[1], m)
        rowmsg[...] = m

    def stage_slot(s):
        if s not in EARLY:
            residual(s, 1 - core, stage.at[s])
        send(("res", s), stage.at[s], res.at[s, pl.ds(B, B)], dc=1)

    def keep_slot(s):
        if s not in own_rows:
            own_rows[s] = residual(s, core, res.at[s, pl.ds(0, B)])

    def zsend(d, way, name):
        s = 0 if d == 1 else OFF.index(way * (d - 1))
        t = 7 if d == 4 else OFF.index(way * d)
        if name == "x":
            half = 32 if d == 4 and way < 0 else 0
            r0, nr, c0, nc = pl.multiple_of(64 * x + half, 32), 32 if d == 4 else 64, AX0, AXN
        else:
            if d == 4 and (name == 0) != (way > 0):
                return
            r0, nr, c0, nc = 128 * name, 128, AZ0, AZN
        send(("az", d, way, name), tab.at[s, pl.ds(r0, nr), pl.ds(c0, nc)],
             tab.at[t, pl.ds(r0, nr), pl.ds(c0, nc)], dz=-way)

    def zhop(d, way, name):
        got(("az", d, way, name))
        zsend(d + 1, way, name)

    def znear(s, name):
        if s == 7:
            got_all([("az", 4, way, name) for way in (1, -1) if ("az", 4, way, name) in made])
        else:
            got(("az", abs(OFF[s]), 1 if OFF[s] > 0 else -1, name))

    def xdirect(s):
        znear(s, "x")
        p = tab.at[s, pl.ds(pl.multiple_of(64 * x, 64), 64), pl.ds(AX0, AXN)]
        for j in (2, 1, 3):
            send(("ax", s, j), p, p, dx=j)

    def table_ready(s):
        if s == 0:
            return
        znear(s, 0)
        znear(s, 1)
        got_all([("ax", s, j) for j in (1, 2, 3)])

    lane = lax.broadcasted_iota(jnp.int32, (1, 128), 1)

    def compute(s):
        table_ready(s)
        if s == 0:
            got("rows")
        got(("res", s))
        r = res.at[s]
        f = tab[s]
        st = lax.dot_general(f, r[...], (((1,), (1,)), ((), ())), preferred_element_type=F32)
        ff = f.astype(F32)
        norm = jnp.sum(ff * ff, axis=1, keepdims=True)
        logits = st * (2.0 / 32.0) - norm * (1.0 / 32.0)
        e = jnp.exp(logits - jnp.max(logits, axis=0, keepdims=True))
        n = own_rows[s]
        n2 = rowin[pl.ds(s, 1), :]
        live = jnp.concatenate([lane < n, lane + 128 < n, lane < n2, lane + 128 < n2], axis=1)
        live = jnp.where(live, 1.0, 0.0)
        w = e * (live / jnp.sum(e, axis=0, keepdims=True))
        wh = w.astype(BF)
        ones = jnp.ones((16, 2 * B), BF)
        cnt = lax.dot_general(ones, wh, (((1,), (1,)), ((), ())), preferred_element_type=F32)
        lhs = jnp.concatenate([wh, jnp.broadcast_to(live, (16, 2 * B)).astype(BF)], axis=0)
        sub = lax.broadcasted_iota(jnp.int32, (8, 128), 0)
        drift = jnp.zeros((8, 128), F32)
        for c0 in range(0, D, 256):
            p = jnp.dot(lhs, r[:, c0:c0 + 256], preferred_element_type=F32)
            for c in (0, 128):
                drift = jnp.where(sub == (c0 + c) // 128, p[K:K + 8, c:c + 128], drift)
            if s not in FAR:
                for yy in range(NY):
                    q = jnp.concatenate([p[64 * k + 8 * yy:64 * k + 8 * yy + 8] for k in range(NX)], axis=0)
                    py[s, yy, :, c0:c0 + 256] = q.astype(BF)
            else:
                for xx in range(NX):
                    px[s - FAR[0], xx, :, c0:c0 + 256] = p[64 * xx:64 * xx + 64].astype(BF)
        seen = jnp.broadcast_to((n + n2).astype(F32), (8, 128))
        more = jnp.where(sub == 0, cnt[:8, :128], jnp.where(sub == 1, cnt[:8, 128:], seen))
        aux[s, 0:8, :] = drift
        aux[s, 8:16, :] = more
        if s:
            send(("auxz", s), aux.at[s], raz.at[s], dz=OFF[s])
        if s in FAR:
            rs_x(s - FAR[0])

    def rs_x(f):
        for j in (2, 1, 3):
            send(("rx", f, j), px.at[f, lax.rem(x + j, NX)], rx.at[f, j - 1], dx=j)

    def rs_x_done(f):
        v = px[f, x].astype(F32)
        for j in (1, 3, 2):
            got(("rx", f, j))
            v = v + rx[f, j - 1].astype(F32)
        for yy in range(NY):
            w = v[8 * yy:8 * yy + 8]
            sbx[f, yy] = jnp.concatenate([w[:, :H], w[:, H:]], axis=0).astype(BF)
        for j in (4, 3, 5, 2, 6, 1, 7):
            send(("bx", f, j), sbx.at[f, lax.rem(y + j, NY)], rbx.at[f, j - 1], dy=j)

    def rs_far_done(f):
        v = sbx[f, y].astype(F32)
        for j in range(1, NY):
            got(("bx", f, j))
            v = v + rbx[f, j - 1].astype(F32)
        szc[f] = v.astype(BF)
        send(("zc", f), szc.at[f], rzc.at[f], dz=OFF[f + FAR[0]])

    def rs_y_slots(g, dist, way):
        sl = GROUPS[g]
        if dist == 4:
            sl = sl[:1] if way > 0 else sl[1:]
        return sl

    def rs_y_send(g, dist, ways=(1, -1)):
        for way in ways:
            sl = rs_y_slots(g, dist, way)
            if not sl:
                continue
            to = lax.rem(y + way * dist + NY, NY)
            send(("ry", g, dist, way), py.at[pl.ds(sl[0], len(sl)), to],
                 ry.at[(way < 0) * 4 + dist - 1, pl.ds(sl[0], len(sl))], dy=way)

    def rs_y_hop(g, dist):
        for way in (1, -1):
            if ("ry", g, dist, way) in made:
                got(("ry", g, dist, way))
                to = lax.rem(y + way * (dist - 1) + NY, NY)
                for s in rs_y_slots(g, dist, way):
                    v = py[s, to].astype(F32) + ry[(way < 0) * 4 + dist - 1, s].astype(F32)
                    py[s, to] = v.astype(BF)
            rs_y_send(g, dist - 1, (way,))

    def rs_y_done(g):
        got_all([("ry", g, 1, 1), ("ry", g, 1, -1)])
        for s in GROUPS[g]:
            rs_y_out(s, py[s, y].astype(F32) + ry[0, s].astype(F32) + ry[4, s].astype(F32))

    def rs_y_out(s, v):
        if s == 0:
            accy[...] = v.reshape(NX, 8, D)
        else:
            szy[s] = v.astype(BF)
            send(("zy", s), szy.at[s], rzy.at[s], dz=OFF[s])

    def add_z(s):
        got(("zy", s))
        accy[...] += rzy[s].astype(F32).reshape(NX, 8, D)

    def last_send():
        for j in (2, 1, 3):
            send(("fy", j), accy.at[lax.rem(x + j, NX)], rfy.at[j - 1], dx=j)

    def aux_z():
        v = aux[0]
        for s in range(1, SLOTS):
            got(("auxz", s))
            v = v + raz[s]
        raz[0] = v
        ray[y] = v
        for j in (4, 3, 5, 2, 6, 1, 7):
            send(("auxy", j), raz.at[0], ray.at[y], dy=j)

    def aux_y():
        got_all([("auxy", j) for j in range(1, NY)])
        v = ray[0]
        for j in range(1, NY):
            v = v + ray[j]
        aux[0] = v
        rax[x] = v
        for j in (2, 1, 3):
            send(("auxx", j), aux.at[0], rax.at[x], dx=j)

    def aux_x():
        got_all([("auxx", j) for j in range(1, NX)])
        v = rax[0]
        for j in range(1, NX):
            v = v + rax[j]
        seen = v[10:11, :]
        d = v[0:8] / (seen + 1.0)
        for i in range(8):
            out[8:9, 128 * i:128 * i + 128] = d[i:i + 1]
        k0 = lax.rem(dp, 16) * 8
        line = jnp.where(dp < 16, v[8:9], v[9:10])
        pick = lax.broadcasted_iota(jnp.int32, (8, 128), 1) == k0 + lax.broadcasted_iota(jnp.int32, (8, 128), 0)
        made["cnt"] = jnp.sum(jnp.where(pick, jnp.broadcast_to(line, (8, 128)), 0.0), axis=1, keepdims=True)

    def finish():
        nonlocal sent
        sent = len(started) - 8
        for c in started[:sent]:
            c.wait_send()
        old = tab[0, pl.ds(pl.multiple_of((dp // 2) * 16, 16), 16), :].astype(F32)
        old = jnp.where(lax.rem(dp, 2) == 0, old[:8], old[8:])
        v = old + accy[x]
        for j in (1, 3, 2):
            got(("fy", j))
            v = v + rfy[j - 1]
        got(("zc", 0))
        far = rzc[0].astype(F32)
        for f in range(1, len(FAR)):
            got(("zc", f))
            far = far + rzc[f].astype(F32)
        div = made["cnt"] + 1.0
        out[:8, :H] = (v[:, :H] + far[:8]) / div
        out[:8, H:] = (v[:, H:] + far[8:]) / div

    def run(kind, *a):
        if kind == "pts":
            send("rows", rowmsg, rowin, dc=1)
        elif kind == "zs":
            zsend(*a)
        elif kind == "zf":
            zhop(*a)
        elif kind == "xp":
            xdirect(*a)
        elif kind == "stage":
            stage_slot(*a)
        elif kind == "keep":
            keep_slot(*a)
        elif kind == "comp":
            compute(*a)
        elif kind == "rxd":
            rs_x_done(a[0] - FAR[0])
        elif kind == "bdone":
            rs_far_done(a[0] - FAR[0])
        elif kind == "ry":
            if a[1] == 4:
                rs_y_send(*a)
            else:
                rs_y_hop(a[0], a[1] + 1)
        elif kind == "ryd":
            rs_y_done(*a)
        elif kind == "addz":
            add_z(*a)
        elif kind == "auxz":
            aux_z()
        elif kind == "auxy":
            aux_y()
        elif kind == "auxx":
            aux_x()
        elif kind == "last":
            last_send()
        elif kind == "finish":
            finish()

    fill_rows()
    load_fine.wait()
    load_pts.wait()
    for s in EARLY:
        residual(s, 1 - core, stage.at[s])
        keep_slot(s)
    pl.semaphore_wait(barrier, len(partners))
    for e in ORDER:
        run(*e)
    for c in started[sent:]:
        c.wait_send()


def split(both, new_fine, coarse_shift):
    new_fine[0] = both[:8]
    coarse_shift[...] = both[8:9]


def per_device(points, block_cluster, block_rows, coarse, fine):
    vmem = pl.BlockSpec(memory_space=pltpu.VMEM)
    smem = pl.BlockSpec(memory_space=pltpu.SMEM)
    hbm = pl.BlockSpec(memory_space=pl.ANY)
    far, near = len(FAR), SLOTS - len(FAR)
    both = pl.pallas_call(
        kernel,
        out_shape=jax.ShapeDtypeStruct((16, D), F32),
        in_specs=[smem, smem, hbm, vmem, hbm],
        out_specs=vmem,
        scratch_shapes=[
            pltpu.VMEM((8, B, D), BF),
            pltpu.VMEM((SLOTS, 2 * B, D), BF),
            pltpu.VMEM((SLOTS, B, D), BF),
            pltpu.VMEM((SLOTS, K, D), BF),
            pltpu.VMEM((near, NY, 32, D), BF),
            pltpu.VMEM((far, NX, 64, D), BF),
            pltpu.VMEM((8, near, 32, D), BF),
            pltpu.VMEM((far, NX - 1, 64, D), BF),
            pltpu.VMEM((near, 32, D), BF),
            pltpu.VMEM((near, 32, D), BF),
            pltpu.VMEM((far, NY, 16, H), BF),
            pltpu.VMEM((far, NY - 1, 16, H), BF),
            pltpu.VMEM((far, 16, H), BF),
            pltpu.VMEM((far, 16, H), BF),
            pltpu.VMEM((NX, 8, D), F32),
            pltpu.VMEM((NX - 1, 8, D), F32),
            pltpu.VMEM((8, 128), jnp.int32),
            pltpu.VMEM((8, 128), jnp.int32),
            pltpu.VMEM((SLOTS, 16, 128), F32),
            pltpu.VMEM((SLOTS, 16, 128), F32),
            pltpu.VMEM((NY, 16, 128), F32),
            pltpu.VMEM((NX, 16, 128), F32),
            pltpu.SemaphoreType.DMA((NSEM,)),
            pltpu.SemaphoreType.DMA((NSEM,)),
            pltpu.SemaphoreType.DMA((2,)),
        ],
        compiler_params=pltpu.CompilerParams(
            collective_id=0, has_side_effects=True, vmem_limit_bytes=56 * 1024 * 1024),
        cost_estimate=pl.CostEstimate(flops=8 * 10**9, bytes_accessed=5 * 10**6, transcendentals=10**6),
        name="lloyd",
    )(block_cluster, block_rows, points.reshape(8, B, D), coarse, fine)
    return pl.pallas_call(
        split,
        out_shape=(jax.ShapeDtypeStruct((1, 8, D), F32), jax.ShapeDtypeStruct((1, D), F32)),
        in_specs=[vmem],
        out_specs=(vmem, vmem),
        name="split",
    )(both)


def solution(mesh):
    placed = (
        P(("dp", "list"), None),
        P(("dp", "list")),
        P(("dp", "list")),
        P(),
        P("list", None, None),
    )
    return jax.shard_map(
        per_device,
        mesh=mesh,
        in_specs=placed,
        out_specs=(P("list", "dp", None), P("list", None)),
        check_vma=False,
    )
```

```python
import functools

import jax
import jax.numpy as jnp
from jax import lax
from jax.experimental import pallas as pl
from jax.experimental.pallas import tpu as pltpu
from jax.sharding import PartitionSpec as P

NX, NY, NZ = 4, 8, 8
D, K, B = 1024, 256, 256
SLOTS = 8
OFF = (0, 1, -1, 2, -2, 3, -3, 4)
GROUPS = ((0,), (1, 2), (3, 4), (5, 6), (7,))
AZ0, AZN = 0, 512
AX0, AXN = 512, 512
FAR = (5, 6, 7)
H = D // 2
EARLY = (0, 1, 2)
NSEM = 400
MESH = pl.DeviceIdType.MESH
BF, F32 = jnp.bfloat16, jnp.float32
ORDER = (
    ("zs", 1, -1, "x"), ("zs", 1, 1, "x"), ("zs", 1, -1, 1), ("pts",), ("stage", 0), ("keep", 5), ("stage", 2),
    ("stage", 5), ("keep", 4), ("zs", 1, 1, 1), ("keep", 0), ("stage", 4), ("keep", 6), ("keep", 7), ("keep", 3),
    ("stage", 7), ("stage", 1), ("stage", 3), ("stage", 6), ("xp", 2), ("zf", 1, -1, "x"), ("zf", 1, 1, "x"),
    ("xp", 1), ("zs", 1, -1, 0), ("keep", 2), ("keep", 1), ("comp", 0), ("ry", 0, 4), ("zs", 1, 1, 0),
    ("zf", 1, -1, 1), ("zf", 1, 1, 1), ("zf", 2, -1, "x"), ("xp", 3), ("xp", 4), ("zf", 2, 1, "x"), ("ry", 0, 3),
    ("zf", 1, -1, 0), ("comp", 2), ("zf", 1, 1, 0), ("comp", 1), ("zf", 2, -1, 1), ("ry", 1, 4), ("zf", 2, 1, 1),
    ("ry", 0, 2), ("xp", 6), ("zf", 3, -1, "x"), ("zf", 3, 1, "x"), ("xp", 5), ("zf", 2, -1, 0), ("ry", 1, 3),
    ("zf", 2, 1, 0), ("comp", 4), ("ry", 0, 1), ("comp", 3), ("zf", 3, -1, 1), ("ry", 2, 4), ("xp", 7), ("ry", 1, 2),
    ("comp", 6), ("ryd", 0), ("zf", 3, 1, 0), ("comp", 5), ("ry", 2, 3), ("ry", 1, 1), ("comp", 7), ("ry", 2, 2),
    ("rxd", 6), ("ryd", 1), ("auxz",), ("ry", 2, 1), ("rxd", 5), ("addz", 1), ("addz", 2), ("bdone", 6), ("auxy",),
    ("rxd", 7), ("ryd", 2), ("auxx",), ("bdone", 5), ("addz", 3), ("addz", 4), ("last",), ("bdone", 7), ("finish",),
)

def kernel(clus, rows, points, coarse, fine, out,
           pts, res, stage, tab, py, px, ry, rx, szy, rzy, sbx, rbx, szc, rzc, accy, rfy,
           rowmsg, rowin, aux, raz, ray, rax, ssem, rsem, lsem):
    dp, li = lax.axis_index("dp"), lax.axis_index("list")
    x, y, z, core = dp // NY, dp % NY, li // 2, li % 2

    def at(dx=0, dy=0, dz=0, dc=0):
        xx = lax.rem(x + dx + NX, NX)
        yy = lax.rem(y + dy + NY, NY)
        zz = lax.rem(z + dz + NZ, NZ)
        return (xx * NY + yy, zz * 2 + lax.rem(core + dc, 2))

    load_pts = pltpu.make_async_copy(points, pts, lsem.at[0])
    load_pts.start()
    load_fine = pltpu.make_async_copy(fine.at[0], tab.at[0], lsem.at[1])
    load_fine.start()

    partners = [dict(dc=1)]
    partners += [dict(dz=d) for d in range(1, NZ)]
    partners += [dict(dy=d) for d in range(1, NY)]
    partners += [dict(dx=d) for d in range(1, NX)]
    barrier = pltpu.get_barrier_semaphore()
    for p in partners:
        pl.semaphore_signal(barrier, inc=1, device_id=at(**p), device_id_type=MESH)

    started = []
    made = {}
    sent = 0

    def send(key, src, dst, **to):
        i = len(made)
        c = pltpu.make_async_remote_copy(
            src_ref=src, dst_ref=dst, send_sem=ssem.at[i], recv_sem=rsem.at[i],
            device_id=at(**to), device_id_type=MESH)
        assert key not in made
        made[key] = c
        c.start()
        started.append(c)

    waited = set()

    def got(key):
        if key not in waited:
            waited.add(key)
            made[key].wait_recv()

    def got_all(keys):
        for k in keys:
            got(k)

    def group_of(s):
        return [s in g for g in GROUPS].index(True)

    cents = coarse[...].astype(F32)
    crow = lax.broadcasted_iota(jnp.int32, (16, 1), 0)

    def find(s, parity):
        c = 2 * lax.rem(z + OFF[s] + NZ, NZ) + parity
        b, n = jnp.int32(0), jnp.int32(0)
        for j in range(8):
            hit = clus[j] == c
            b = jnp.where(hit, j, b)
            n = jnp.where(hit, rows[j], n)
        centre = jnp.sum(jnp.where(crow == c, cents, 0.0), axis=0, keepdims=True)
        return b, n, centre

    def residual(s, parity, put):
        b, n, centre = find(s, parity)

        @pl.loop(0, B, step=32)
        def _(r):
            r = pl.multiple_of(r, 32)
            v = pts[b, pl.ds(r, 32), :].astype(F32) - centre
            put[pl.ds(r, 32), :] = v.astype(BF)

        return n

    own_rows = {}

    def fill_rows():
        sub = lax.broadcasted_iota(jnp.int32, (8, 128), 0)
        m = jnp.zeros((8, 128), jnp.int32)
        for s in range(SLOTS):
            m = jnp.where(sub == s, find(s, 1 - core)[1], m)
        rowmsg[...] = m

    def stage_slot(s):
        if s not in EARLY:
            residual(s, 1 - core, stage.at[s])
        send(("res", s), stage.at[s], res.at[s, pl.ds(B, B)], dc=1)

    def keep_slot(s):
        if s not in own_rows:
            own_rows[s] = residual(s, core, res.at[s, pl.ds(0, B)])

    def zsend(d, way, name):
        s = 0 if d == 1 else OFF.index(way * (d - 1))
        t = 7 if d == 4 else OFF.index(way * d)
        if name == "x":
            half = 32 if d == 4 and way < 0 else 0
            r0, nr, c0, nc = pl.multiple_of(64 * x + half, 32), 32 if d == 4 else 64, AX0, AXN
        else:
            if d == 4 and (name == 0) != (way > 0):
                return
            r0, nr, c0, nc = 128 * name, 128, AZ0, AZN
        send(("az", d, way, name), tab.at[s, pl.ds(r0, nr), pl.ds(c0, nc)],
             tab.at[t, pl.ds(r0, nr), pl.ds(c0, nc)], dz=-way)

    def zhop(d, way, name):
        got(("az", d, way, name))
        zsend(d + 1, way, name)

    def znear(s, name):
        if s == 7:
            got_all([("az", 4, way, name) for way in (1, -1) if ("az", 4, way, name) in made])
        else:
            got(("az", abs(OFF[s]), 1 if OFF[s] > 0 else -1, name))

    def xdirect(s):
        znear(s, "x")
        p = tab.at[s, pl.ds(pl.multiple_of(64 * x, 64), 64), pl.ds(AX0, AXN)]
        for j in (2, 1, 3):
            send(("ax", s, j), p, p, dx=j)

    def table_ready(s):
        if s == 0:
            return
        znear(s, 0)
        znear(s, 1)
        got_all([("ax", s, j) for j in (1, 2, 3)])

    lane = lax.broadcasted_iota(jnp.int32, (1, 128), 1)

    def compute(s):
        table_ready(s)
        if s == 0:
            got("rows")
        got(("res", s))
        r = res.at[s]
        f = tab[s]
        st = lax.dot_general(f, r[...], (((1,), (1,)), ((), ())), preferred_element_type=F32)
        ff = f.astype(F32)
        norm = jnp.sum(ff * ff, axis=1, keepdims=True)
        logits = st * (2.0 / 32.0) - norm * (1.0 / 32.0)
        e = jnp.exp(logits - jnp.max(logits, axis=0, keepdims=True))
        n = own_rows[s]
        n2 = rowin[pl.ds(s, 1), :]
        live = jnp.concatenate([lane < n, lane + 128 < n, lane < n2, lane + 128 < n2], axis=1)
        live = jnp.where(live, 1.0, 0.0)
        w = e * (live / jnp.sum(e, axis=0, keepdims=True))
        wh = w.astype(BF)
        ones = jnp.ones((16, 2 * B), BF)
        cnt = lax.dot_general(ones, wh, (((1,), (1,)), ((), ())), preferred_element_type=F32)
        lhs = jnp.concatenate([wh, jnp.broadcast_to(live, (16, 2 * B)).astype(BF)], axis=0)
        sub = lax.broadcasted_iota(jnp.int32, (8, 128), 0)
        drift = jnp.zeros((8, 128), F32)
        for c0 in range(0, D, 256):
            p = jnp.dot(lhs, r[:, c0:c0 + 256], preferred_element_type=F32)
            for c in (0, 128):
                drift = jnp.where(sub == (c0 + c) // 128, p[K:K + 8, c:c + 128], drift)
            if s not in FAR:
                for yy in range(NY):
                    q = jnp.concatenate([p[64 * k + 8 * yy:64 * k + 8 * yy + 8] for k in range(NX)], axis=0)
                    py[s, yy, :, c0:c0 + 256] = q.astype(BF)
            else:
                for xx in range(NX):
                    px[s - FAR[0], xx, :, c0:c0 + 256] = p[64 * xx:64 * xx + 64].astype(BF)
        seen = jnp.broadcast_to((n + n2).astype(F32), (8, 128))
        more = jnp.where(sub == 0, cnt[:8, :128], jnp.where(sub == 1, cnt[:8, 128:], seen))
        aux[s, 0:8, :] = drift
        aux[s, 8:16, :] = more
        if s:
            send(("auxz", s), aux.at[s], raz.at[s], dz=OFF[s])
        if s in FAR:
            rs_x(s - FAR[0])

    def rs_x(f):
        for j in (2, 1, 3):
            send(("rx", f, j), px.at[f, lax.rem(x + j, NX)], rx.at[f, j - 1], dx=j)

    def rs_x_done(f):
        v = px[f, x].astype(F32)
        for j in (1, 3, 2):
            got(("rx", f, j))
            v = v + rx[f, j - 1].astype(F32)
        for yy in range(NY):
            w = v[8 * yy:8 * yy + 8]
            sbx[f, yy] = jnp.concatenate([w[:, :H], w[:, H:]], axis=0).astype(BF)
        for j in (4, 3, 5, 2, 6, 1, 7):
            send(("bx", f, j), sbx.at[f, lax.rem(y + j, NY)], rbx.at[f, j - 1], dy=j)

    def rs_far_done(f):
        v = sbx[f, y].astype(F32)
        for j in range(1, NY):
            got(("bx", f, j))
            v = v + rbx[f, j - 1].astype(F32)
        szc[f] = v.astype(BF)
        send(("zc", f), szc.at[f], rzc.at[f], dz=OFF[f + FAR[0]])

    def rs_y_slots(g, dist, way):
        sl = GROUPS[g]
        if dist == 4:
            sl = sl[:1] if way > 0 else sl[1:]
        return sl

    def rs_y_send(g, dist, ways=(1, -1)):
        for way in ways:
            sl = rs_y_slots(g, dist, way)
            if not sl:
                continue
            to = lax.rem(y + way * dist + NY, NY)
            send(("ry", g, dist, way), py.at[pl.ds(sl[0], len(sl)), to],
                 ry.at[(way < 0) * 4 + dist - 1, pl.ds(sl[0], len(sl))], dy=way)

    def rs_y_hop(g, dist):
        for way in (1, -1):
            if ("ry", g, dist, way) in made:
                got(("ry", g, dist, way))
                to = lax.rem(y + way * (dist - 1) + NY, NY)
                for s in rs_y_slots(g, dist, way):
                    v = py[s, to].astype(F32) + ry[(way < 0) * 4 + dist - 1, s].astype(F32)
                    py[s, to] = v.astype(BF)
            rs_y_send(g, dist - 1, (way,))

    def rs_y_done(g):
        got_all([("ry", g, 1, 1), ("ry", g, 1, -1)])
        for s in GROUPS[g]:
            rs_y_out(s, py[s, y].astype(F32) + ry[0, s].astype(F32) + ry[4, s].astype(F32))

    def rs_y_out(s, v):
        if s == 0:
            accy[...] = v.reshape(NX, 8, D)
        else:
            szy[s] = v.astype(BF)
            send(("zy", s), szy.at[s], rzy.at[s], dz=OFF[s])

    def add_z(s):
        got(("zy", s))
        accy[...] += rzy[s].astype(F32).reshape(NX, 8, D)

    def last_send():
        for j in (2, 1, 3):
            send(("fy", j), accy.at[lax.rem(x + j, NX)], rfy.at[j - 1], dx=j)

    def aux_z():
        v = aux[0]
        for s in range(1, SLOTS):
            got(("auxz", s))
            v = v + raz[s]
        raz[0] = v
        ray[y] = v
        for j in (4, 3, 5, 2, 6, 1, 7):
            send(("auxy", j), raz.at[0], ray.at[y], dy=j)

    def aux_y():
        got_all([("auxy", j) for j in range(1, NY)])
        v = ray[0]
        for j in range(1, NY):
            v = v + ray[j]
        aux[0] = v
        rax[x] = v
        for j in (2, 1, 3):
            send(("auxx", j), aux.at[0], rax.at[x], dx=j)

    def aux_x():
        got_all([("auxx", j) for j in range(1, NX)])
        v = rax[0]
        for j in range(1, NX):
            v = v + rax[j]
        seen = v[10:11, :]
        d = v[0:8] / (seen + 1.0)
        for i in range(8):
            out[8:9, 128 * i:128 * i + 128] = d[i:i + 1]
        k0 = lax.rem(dp, 16) * 8
        line = jnp.where(dp < 16, v[8:9], v[9:10])
        pick = lax.broadcasted_iota(jnp.int32, (8, 128), 1) == k0 + lax.broadcasted_iota(jnp.int32, (8, 128), 0)
        made["cnt"] = jnp.sum(jnp.where(pick, jnp.broadcast_to(line, (8, 128)), 0.0), axis=1, keepdims=True)

    def finish():
        nonlocal sent
        sent = len(started) - 8
        for c in started[:sent]:
            c.wait_send()
        old = tab[0, pl.ds(pl.multiple_of((dp // 2) * 16, 16), 16), :].astype(F32)
        old = jnp.where(lax.rem(dp, 2) == 0, old[:8], old[8:])
        v = old + accy[x]
        for j in (1, 3, 2):
            got(("fy", j))
            v = v + rfy[j - 1]
        got(("zc", 0))
        far = rzc[0].astype(F32)
        for f in range(1, len(FAR)):
            got(("zc", f))
            far = far + rzc[f].astype(F32)
        div = made["cnt"] + 1.0
        out[:8, :H] = (v[:, :H] + far[:8]) / div
        out[:8, H:] = (v[:, H:] + far[8:]) / div

    def run(kind, *a):
        if kind == "pts":
            send("rows", rowmsg, rowin, dc=1)
        elif kind == "zs":
            zsend(*a)
        elif kind == "zf":
            zhop(*a)
        elif kind == "xp":
            xdirect(*a)
        elif kind == "stage":
            stage_slot(*a)
        elif kind == "keep":
            keep_slot(*a)
        elif kind == "comp":
            compute(*a)
        elif kind == "rxd":
            rs_x_done(a[0] - FAR[0])
        elif kind == "bdone":
            rs_far_done(a[0] - FAR[0])
        elif kind == "ry":
            if a[1] == 4:
                rs_y_send(*a)
            else:
                rs_y_hop(a[0], a[1] + 1)
        elif kind == "ryd":
            rs_y_done(*a)
        elif kind == "addz":
            add_z(*a)
        elif kind == "auxz":
            aux_z()
        elif kind == "auxy":
            aux_y()
        elif kind == "auxx":
            aux_x()
        elif kind == "last":
            last_send()
        elif kind == "finish":
            finish()

    fill_rows()
    load_fine.wait()
    load_pts.wait()
    for s in EARLY:
        residual(s, 1 - core, stage.at[s])
        keep_slot(s)
    pl.semaphore_wait(barrier, len(partners))
    for e in ORDER:
        run(*e)
    for c in started[sent:]:
        c.wait_send()


def split(both, new_fine, coarse_shift):
    new_fine[0] = both[:8]
    coarse_shift[...] = both[8:9]


def per_device(points, block_cluster, block_rows, coarse, fine):
    vmem = pl.BlockSpec(memory_space=pltpu.VMEM)
    smem = pl.BlockSpec(memory_space=pltpu.SMEM)
    hbm = pl.BlockSpec(memory_space=pl.ANY)
    far, near = len(FAR), SLOTS - len(FAR)
    both = pl.pallas_call(
        kernel,
        out_shape=jax.ShapeDtypeStruct((16, D), F32),
        in_specs=[smem, smem, hbm, vmem, hbm],
        out_specs=vmem,
        scratch_shapes=[
            pltpu.VMEM((8, B, D), BF),
            pltpu.VMEM((SLOTS, 2 * B, D), BF),
            pltpu.VMEM((SLOTS, B, D), BF),
            pltpu.VMEM((SLOTS, K, D), BF),
            pltpu.VMEM((near, NY, 32, D), BF),
            pltpu.VMEM((far, NX, 64, D), BF),
            pltpu.VMEM((8, near, 32, D), BF),
            pltpu.VMEM((far, NX - 1, 64, D), BF),
            pltpu.VMEM((near, 32, D), BF),
            pltpu.VMEM((near, 32, D), BF),
            pltpu.VMEM((far, NY, 16, H), BF),
            pltpu.VMEM((far, NY - 1, 16, H), BF),
            pltpu.VMEM((far, 16, H), BF),
            pltpu.VMEM((far, 16, H), BF),
            pltpu.VMEM((NX, 8, D), F32),
            pltpu.VMEM((NX - 1, 8, D), F32),
            pltpu.VMEM((8, 128), jnp.int32),
            pltpu.VMEM((8, 128), jnp.int32),
            pltpu.VMEM((SLOTS, 16, 128), F32),
            pltpu.VMEM((SLOTS, 16, 128), F32),
            pltpu.VMEM((NY, 16, 128), F32),
            pltpu.VMEM((NX, 16, 128), F32),
            pltpu.SemaphoreType.DMA((NSEM,)),
            pltpu.SemaphoreType.DMA((NSEM,)),
            pltpu.SemaphoreType.DMA((2,)),
        ],
        compiler_params=pltpu.CompilerParams(
            collective_id=0, has_side_effects=True, vmem_limit_bytes=56 * 1024 * 1024),
        cost_estimate=pl.CostEstimate(flops=8 * 10**9, bytes_accessed=5 * 10**6, transcendentals=10**6),
        name="lloyd",
    )(block_cluster, block_rows, points.reshape(8, B, D), coarse, fine)
    return pl.pallas_call(
        split,
        out_shape=(jax.ShapeDtypeStruct((1, 8, D), F32), jax.ShapeDtypeStruct((1, D), F32)),
        in_specs=[vmem],
        out_specs=(vmem, vmem),
        name="split",
    )(both)


def solution(mesh):
    placed = (
        P(("dp", "list"), None),
        P(("dp", "list")),
        P(("dp", "list")),
        P(),
        P("list", None, None),
    )
    return jax.shard_map(
        per_device,
        mesh=mesh,
        in_specs=placed,
        out_specs=(P("list", "dp", None), P("list", None)),
        check_vma=False,
    )
```
